32 devices in a mesh: ctx: 16 (over z, y, core), tp: 2 (over x).
Axes of the slice: x: 2, y: 2, z: 4, core: 2. Of those that a mesh axis runs over, the one named last changes fastest.
Arguments:
- inputs: bfloat16 [3072, 2048], P('ctx'), may hold values from -8 to 8
- norm1_gain: float32 [2048], replicated, may hold values from 0.1 to 1.9
- query_weight: bfloat16 [2048, 2048], P('ctx', 'tp'), may hold values from -0.125 to 0.125
- key_weight: bfloat16 [2048, 512], P('ctx', 'tp'), may hold values from -0.125 to 0.125
- value_weight: bfloat16 [2048, 512], P('ctx', 'tp'), may hold values from -0.125 to 0.125
- query_gain: float32 [64], replicated, may hold values from 0.1 to 1.9
- key_gain: float32 [64], replicated, may hold values from 0.1 to 1.9
- out_weight: bfloat16 [2048, 2048], P('tp', 'ctx'), may hold values from -3 to 3
- norm2_gain: float32 [2048], replicated, may hold values from 0.1 to 1.9
- gate_weight: bfloat16 [2048, 8192], P('ctx', 'tp'), may hold values from -0.125 to 0.125
- up_weight: bfloat16 [2048, 8192], P('ctx', 'tp'), may hold values from -0.125 to 0.125
- down_weight: bfloat16 [8192, 2048], P('tp', 'ctx'), may hold values from -0.0625 to 0.0625
- doc_starts: int32 [4], replicated, may hold values from 0 to 3071, as said below
- cotangent: bfloat16 [3072, 2048], P('ctx'), may hold values from -8 to 8
Outputs:
- output: bfloat16 [3072, 2048], P('ctx')
- input_grad: bfloat16 [3072, 2048], P('ctx')
- norm1_grad: float32 [2048], replicated
- query_grad: float32 [2048, 2048], P('ctx', 'tp')
- key_grad: float32 [2048, 512], P('ctx', 'tp')
- value_grad: float32 [2048, 512], P('ctx', 'tp')
- query_gain_grad: float32 [64], replicated
- key_gain_grad: float32 [64], replicated
- out_grad: float32 [2048, 2048], P('tp', 'ctx')
- norm2_grad: float32 [2048], replicated
- gate_grad: float32 [2048, 8192], P('ctx', 'tp')
- up_grad: float32 [2048, 8192], P('ctx', 'tp')
- down_grad: float32 [8192, 2048], P('tp', 'ctx')
The draws below stay inside these ranges and needn't reach their ends.
Inputs may be any that keep to these rules, and one draw needn't show every extreme that they name: `doc_starts`: strictly increasing; the first entry is 0, the second lies in 1 .. 191, the third in 2881 .. 2975 and the fourth in 2976 .. 3071.
All inputs are finite; a program needn't handle non-finite values.
Results may differ from the reference program's by a relative error of at most 0.018.
Values may be sent and summed in bfloat16 or wider, within the bound.
No kernel may reach another device: no remote copies, remote signals or barrier semaphores. Data moves between devices by JAX's collectives and lax.ppermute only.
A program may use at most 248 MiB of HBM per device.

```python
import jax
import jax.numpy as jnp
from jax import lax

D = 2048
QUERY_HEAD_COUNT = 32
SHARED_KV_HEADS = 8
HEAD_SIZE = 64
FF = 8192
TOKENS_PER_PART = 192
QD = 2048
KD = 512
SEQUENCE_TOKENS = 3072


def draw_doc_starts(key, part):
    key = jax.random.fold_in(key, 7)
    first_key, second_key, third_key = jax.random.split(key, 3)
    early_start = jax.random.randint(first_key, (1,), 1, TOKENS_PER_PART)
    late_start = SEQUENCE_TOKENS - TOKENS_PER_PART + jax.random.randint(second_key, (1,), 1, TOKENS_PER_PART // 2)
    final_start = SEQUENCE_TOKENS - TOKENS_PER_PART // 2 + jax.random.randint(third_key, (1,), 0, TOKENS_PER_PART // 2)
    return jnp.concatenate([jnp.zeros((1,), jnp.int32), early_start, late_start, final_start]).astype(jnp.int32)


def spiked(values, rng, source, target, shards_of, factor):
    def block_of(axis_at):
        return (jnp.arange(values.shape[axis_at]) // (values.shape[axis_at] // shards_of)).reshape((-1,) + (1,) * (values.ndim - 1 - axis_at))

    first = jax.random.permutation(rng, shards_of)[block_of(target)]
    second = (block_of(target) + shards_of // 2) % shards_of
    return jnp.where((block_of(source) == first) | (block_of(source) == second), factor * values, values)


def steps_of(key, extent, cuts, smallest, largest):
    factor_of, own = 1.0, jax.random.fold_in(key, 6)
    for axis_at, shards_of in cuts:
        heights = jnp.exp(jax.random.uniform(jax.random.fold_in(own, axis_at), (shards_of,), jnp.float32, smallest / len(cuts), largest / len(cuts)))
        factor_of = factor_of * jnp.repeat(heights, extent[axis_at] // shards_of).reshape([-1 if axis == axis_at else 1 for axis in range(len(extent))])
    return factor_of


def noise(key, extent, scale, most, cuts=(), kind=jnp.bfloat16):
    entries = scale * jax.random.normal(key, extent, jnp.float32)
    if cuts:
        entries = entries * steps_of(key, extent, cuts, -0.22, 0.18)
    return jnp.clip(entries, -most, most).astype(kind)


def noise_with(rng, extent, width, reach, pieces, heavy, kind=jnp.bfloat16):
    values = width * jax.random.normal(rng, extent, jnp.float32)
    if pieces:
        values = values * steps_of(rng, extent, pieces, -0.22, 0.18)
    return jnp.clip(spiked(values, jax.random.fold_in(rng, 3), *heavy), -reach, reach).astype(kind)


def setup_inputs(seed: int = 0) -> dict:
    arg_keys = jax.random.split(jax.random.key(seed), 15)
    return {
        "inputs": noise_with(arg_keys[0], (SEQUENCE_TOKENS, D), 1.0, 8.0, ((0, 16),), (0, 1, 16, 2.0)),
        "norm1_gain": jnp.clip(1.0 + 0.18 * jax.random.normal(arg_keys[1], (D,), jnp.float32), 0.1, 1.9),
        "query_weight": noise(arg_keys[2], (D, QD), D ** -0.5, 0.125, ((0, 16), (1, 2))),
        "key_weight": noise(arg_keys[3], (D, KD), D ** -0.5, 0.125, ((0, 16), (1, 2))),
        "value_weight": noise(arg_keys[4], (D, KD), D ** -0.5, 0.125, ((0, 16), (1, 2))),
        "query_gain": jnp.clip(1.0 + 0.18 * jax.random.normal(arg_keys[5], (HEAD_SIZE,), jnp.float32), 0.1, 1.9),
        "key_gain": jnp.clip(1.0 + 0.18 * jax.random.normal(arg_keys[6], (HEAD_SIZE,), jnp.float32), 0.1, 1.9),
        "out_weight": noise(arg_keys[7], (QD, D), 0.5, 3.0, ((0, 2), (1, 16))),
        "norm2_gain": jnp.clip(1.0 + 0.18 * jax.random.normal(arg_keys[8], (D,), jnp.float32), 0.1, 1.9),
        "gate_weight": noise(arg_keys[9], (D, FF), D ** -0.5, 0.125, ((0, 16), (1, 2))),
        "up_weight": noise(arg_keys[10], (D, FF), D ** -0.5, 0.125, ((0, 16), (1, 2))),
        "down_weight": noise(arg_keys[11], (FF, D), FF ** -0.5, 0.0625, ((0, 2), (1, 16))),
        "doc_starts": draw_doc_starts(jax.random.fold_in(arg_keys[14], 71), 0),
        "cotangent": noise_with(arg_keys[13], (SEQUENCE_TOKENS, D), 1.0, 8.0, ((0, 16),), (0, 1, 16, 2.0)),
    }


epsilon = 1e-05
rope_base = 1000000.0
neg_large = -1e+30
highest = lax.Precision.HIGHEST

@jax.custom_vjp
def reduced_precision(v):
    return lax.optimization_barrier(v.astype(jnp.bfloat16)).astype(jnp.float32)

@jax.custom_vjp
def reduced_backward(v):
    return v

def low_keep(v):
    return (reduced_precision(v), None)

def low_pass(kept, grad):
    return (grad,)

def back_keep(v):
    return (v, None)

def back_low(kept, grad):
    return (reduced_precision(grad),)
reduced_precision.defvjp(low_keep, low_pass)
reduced_backward.defvjp(back_keep, back_low)

def norm_rows(values, gain):
    inverse = lax.rsqrt(lax.optimization_barrier(jnp.mean(values * values, axis=-1, keepdims=True)) + epsilon)
    return values * inverse * gain

def angles(positions, head_width):
    half_width = head_width // 2
    ladder = jnp.arange(half_width, dtype=jnp.float32)
    freq_table = 1.0 / rope_base ** (ladder * 2.0 / head_width)
    turned = positions.astype(jnp.float32)[:, None] * freq_table[None, :]
    return (jnp.cos(turned)[:, None, :], jnp.sin(turned)[:, None, :])

def rotate(values, cosine, sine_table):
    half_width = values.shape[-1] // 2
    first_half = values[..., :half_width]
    second_half = values[..., half_width:]
    return jnp.concatenate([first_half * cosine - second_half * sine_table, second_half * cosine + first_half * sine_table], axis=-1)

def document_info(positions, starts):
    inside = starts[None, :] <= positions[:, None]
    ident = lax.optimization_barrier(jnp.sum(inside.astype(jnp.int32), axis=1)) - 1
    begin = lax.optimization_barrier(jnp.max(jnp.where(inside, starts[None, :], 0), axis=1))
    return (ident.astype(jnp.int32), (positions - begin).astype(jnp.int32))

def matrix_multiply(left_side, right_side):
    return jnp.dot(left_side, right_side, precision=highest, preferred_element_type=jnp.float32)

def attend_block(query_block, query_place, query_doc, key_row_matrix, value_row_matrix, key_place, key_doc):
    scores = jnp.einsum('tkgd,jkd->kgtj', query_block, key_row_matrix, precision=highest) * HEAD_SIZE ** (-0.5)
    scores = reduced_backward(scores)
    allowed = (key_place[None, :] <= query_place[:, None]) & (key_doc[None, :] == query_doc[:, None])
    allowed = allowed[None, None]
    masked = jnp.where(allowed, scores, neg_large)
    row_top = lax.optimization_barrier(jnp.max(masked, axis=-1, keepdims=True))
    row_total = lax.optimization_barrier(jnp.sum(jnp.where(allowed, jnp.exp(masked - row_top), 0.0), axis=-1, keepdims=True))
    weights = jnp.where(allowed, jnp.exp(masked - (row_top + jnp.log(row_total))), 0.0)
    return jnp.einsum('kgtj,jkd->tkgd', reduced_precision(weights), value_row_matrix, precision=highest)

def reference(inputs, norm1_gain, query_weight, key_weight, value_weight, query_gain, key_gain, out_weight, norm2_gain, gate_weight, up_weight, down_weight, doc_starts, cotangent):
    positions = jnp.arange(SEQUENCE_TOKENS, dtype=jnp.int32)
    doc_ids, relative = document_info(positions, doc_starts)
    cosine, sine_table = angles(relative, HEAD_SIZE)
    heads_per_group = QUERY_HEAD_COUNT // SHARED_KV_HEADS
    number_of_blocks = SEQUENCE_TOKENS // TOKENS_PER_PART

    def layer(in_float, gain_one, w_query, key_projection_weight, value_projection_weight, g_query, g_key, w_out, gain_two, w_gate, w_up, w_down):
        first_normalized = reduced_precision(norm_rows(in_float, gain_one))
        query_rows_all = reduced_backward(matrix_multiply(first_normalized, w_query)).reshape(SEQUENCE_TOKENS, QUERY_HEAD_COUNT, HEAD_SIZE)
        key_row_matrix = reduced_backward(matrix_multiply(first_normalized, key_projection_weight)).reshape(SEQUENCE_TOKENS, SHARED_KV_HEADS, HEAD_SIZE)
        value_row_matrix = reduced_precision(reduced_backward(matrix_multiply(first_normalized, value_projection_weight))).reshape(SEQUENCE_TOKENS, SHARED_KV_HEADS, HEAD_SIZE)
        query_rows_all = reduced_precision(rotate(norm_rows(query_rows_all, g_query), cosine, sine_table))
        key_row_matrix = reduced_precision(rotate(norm_rows(key_row_matrix, g_key), cosine, sine_table))
        query_block_list = query_rows_all.reshape(number_of_blocks, TOKENS_PER_PART, SHARED_KV_HEADS, heads_per_group, HEAD_SIZE)
        place_blocks = positions.reshape(number_of_blocks, TOKENS_PER_PART)
        doc_blocks = doc_ids.reshape(number_of_blocks, TOKENS_PER_PART)

        def one_block(element):
            return attend_block(element[0], element[1], element[2], key_row_matrix, value_row_matrix, positions, doc_ids)
        mixed_heads = lax.map(jax.checkpoint(one_block), (query_block_list, place_blocks, doc_blocks))
        mixed_heads = reduced_precision(reduced_backward(mixed_heads.reshape(SEQUENCE_TOKENS, QD)))
        attended = reduced_backward(matrix_multiply(mixed_heads, w_out))
        middle = in_float + attended
        normed_two = reduced_precision(norm_rows(middle, gain_two))
        gate_vals = reduced_backward(matrix_multiply(normed_two, w_gate))
        up_vals = reduced_backward(matrix_multiply(normed_two, w_up))
        hidden = reduced_precision(jax.nn.silu(gate_vals) * up_vals)
        return middle + matrix_multiply(hidden, w_down)
    result, pullback = jax.vjp(layer, inputs.astype(jnp.float32), norm1_gain.astype(jnp.float32), query_weight.astype(jnp.float32), key_weight.astype(jnp.float32), value_weight.astype(jnp.float32), query_gain.astype(jnp.float32), key_gain.astype(jnp.float32), out_weight.astype(jnp.float32), norm2_gain.astype(jnp.float32), gate_weight.astype(jnp.float32), up_weight.astype(jnp.float32), down_weight.astype(jnp.float32))
    grads = pullback(cotangent.astype(jnp.float32))
    return (result.astype(jnp.bfloat16), grads[0].astype(jnp.bfloat16), grads[1], grads[2], grads[3], grads[4], grads[5], grads[6], grads[7], grads[8], grads[9], grads[10], grads[11])
```

```python
import functools

import jax
import jax.numpy as jnp
from jax import lax
from jax.experimental import pallas as pl
from jax.experimental.pallas import tpu as pltpu
from jax.sharding import Mesh
from jax.sharding import PartitionSpec as P

epsilon = 1e-05
rope_base = 1000000.0
RING = 4
QUARTERS = 4
ORDER = (1, 2, 3, 0)
LOG2E = 1.4426950408889634
NEG = -1e30
PAIR = 2
DEPTH = {"a": 2, "b": 1, "tp": 1}
bf16 = jnp.bfloat16
f32 = jnp.float32


def norm_rows(values):
    inverse = lax.rsqrt(jnp.mean(values * values, axis=-1, keepdims=True) + epsilon)
    return values * inverse, inverse


def norm_back(grad_out, gain, unit_rows, inverse):
    scaled = grad_out * gain
    inner_mean = jnp.mean(scaled * unit_rows, axis=-1, keepdims=True)
    return inverse * (scaled - unit_rows * inner_mean)


def dot(left, right, left_dim, right_dim):
    return lax.dot_general(
        left, right, (((left_dim,), (right_dim,)), ((), ())), preferred_element_type=f32
    )


class Links:
    def __init__(self):
        self.sent = {}

    def send(self, link, values, move):
        sent = self.sent.setdefault(link, [])
        if len(sent) >= DEPTH[link]:
            values = lax.optimization_barrier((*values, *sent[-DEPTH[link]]))[: len(values)]
        sent.append(tuple(move(i, value) for i, value in enumerate(values)))
        return sent[-1]


links = Links()


def ring_permute(value, step):
    return lax.ppermute(value, "a", [(i, (i + step) % RING) for i in range(RING)])


def ring_shift(value, step):
    return links.send("a", [value], lambda _, v: ring_permute(v, step))[0]


def swap(value, axis):
    def move(_, v):
        return lax.ppermute(v, axis, [(0, 1), (1, 0)])

    return move(0, value) if axis == "core" else links.send(axis, [value], move)[0]


def after(value, *events):
    return lax.optimization_barrier((value,) + events)[0]


def after_all(values, *events):
    return list(lax.optimization_barrier((*values, *events))[: len(values)])


def window(buffer, index):
    start = [0 if i is None else i for i in index] + [0] * (buffer.ndim - len(index))
    shape = [buffer.shape[d] if i is None else 1 for d, i in enumerate(index)]
    return start, shape + list(buffer.shape[len(index) :])


def put(buffer, value, *index):
    start, shape = window(buffer, index)
    return lax.dynamic_update_slice(buffer, value.reshape(shape), start)


def take(buffer, *index):
    start, shape = window(buffer, index)
    kept = [buffer.shape[d] for d, i in enumerate(index) if i is None]
    return lax.dynamic_slice(buffer, start, shape).reshape(kept + list(buffer.shape[len(index) :]))


class Place:
    def __init__(self, count):
        self.a, self.b, self.core, self.x = (lax.axis_index(n) for n in ("a", "b", "core", "tp"))
        self.count = count

    def back(self, k):
        return (self.a - k) % RING

    def ahead(self, k):
        return (self.a + k) % RING

    def assembled(self, pieces):
        own = jnp.zeros((RING,) + pieces[0].shape, pieces[0].dtype)
        for k in range(RING):
            own = put(own, pieces[k], self.back(k))
        return own.reshape(-1, own.shape[-1])

    def over_b_rows(self, own):
        return swap(own, "b")

    def offsets(self, width):
        quarter = width // QUARTERS
        first = self.b if self.count == 2 else 0
        return [(c * 2 + h) * quarter for c in (self.core, 1 - self.core) for h in (first, 1 - first)]

    def over_b(self, array):
        if self.count == 2:
            theirs = swap(take(array, 1 - self.b).astype(bf16), "b")
            return take(array, self.b) + theirs.astype(f32)
        return lax.psum_scatter(array.astype(bf16), "b", scatter_dimension=0, tiled=False).astype(f32)

    def sum_everywhere(self, value):
        def tree(values):
            while len(values) > 1:
                values = [values[i] + values[i + 1] for i in range(0, len(values), 2)]
            return values[0]

        value = value + swap(value, "core")
        if self.count == 2:
            axes = ("b", "tp")
            value = tree([value] + [lax.ppermute(value, axes, [(i, i ^ m) for i in range(4)]) for m in (1, 2, 3)])
        else:
            value = lax.psum(value, "b")
            value = value + lax.ppermute(value, "tp", [(0, 1), (1, 0)])
        return tree([value] + [lax.ppermute(value, "a", [(i, i ^ m) for i in range(RING)]) for m in range(1, RING)])


class RowGather:
    def __init__(self, own, other=None):
        self.mine, self.other = [own], [] if other is None else [other]

    def ring(self, *due):
        self.mine.append(ring_shift(after(self.mine[-1], *due) if due else self.mine[-1], 1))

    def cross(self):
        self.other.append(swap(self.mine[len(self.other)], "tp"))

    def all(self):
        for _ in range(1, RING):
            self.ring()
            self.cross()
        if len(self.other) < RING:
            self.cross()
        return self

    def chunks(self):
        return list(zip(self.mine, self.other))


class RowScatter:
    def __init__(self):
        self.totals, self.theirs, self.arrived = [], [], []

    def cross(self, mine, other):
        self.theirs.append(swap(other, "tp"))
        self.totals.append(mine.astype(f32) + self.theirs[-1].astype(f32))

    def ring(self):
        n = len(self.arrived)
        self.arrived.append(ring_shift(self.sum(n).astype(bf16), 1))

    def sum(self, n):
        return self.totals[n] + self.arrived[n - 1].astype(f32) if n else self.totals[0]


class Exchange:
    def __init__(self, at, parts):
        self.at, self.parts, self.got, self.hop = at, parts, [take(parts, at.a), None, None, None], None

    def piece(self, k):
        return take(self.parts, self.at.ahead(k))

    def step(self, k):
        if k != 2:
            self.got[k] = ring_shift(self.piece(k), k)
            return
        if self.hop is None:
            self.hop = ring_shift(self.piece(2), 1)
        else:
            self.got[2] = ring_shift(self.hop, 1)

    def steps(self):
        for k in (1, 3, 2, 2):
            self.step(k)
        return [self.got[1], self.got[3], self.hop, self.got[2]]

    def whole(self):
        got = links.send("a", [self.piece(k) for k in (1, 2, 3)], lambda i, v: ring_permute(v, i + 1))
        self.got[1:] = got
        return self.got


def lay_kernel(turned, place_ref, *refs):
    pieces, out_ref = refs[:-1], refs[-1]
    for k, piece in enumerate(pieces):

        @pl.when(pl.program_id(0) == k)
        def _(piece=piece):
            value = piece[...].astype(f32)
            out_ref[...] = value.T if turned else value


def lay(pieces, a, first, n, turned):
    rows = pieces[0].shape[0]
    block = first // n
    place = a
    if turned:
        shape, spec = (RING * n, rows), pl.BlockSpec((n, rows), lambda k, p: ((p[0] + RING - k) % RING, 0))
    else:
        shape, spec = (rows, RING * n), pl.BlockSpec((rows, n), lambda k, p: (0, (p[0] + RING - k) % RING))
    return pl.pallas_call(
        functools.partial(lay_kernel, turned),
        grid_spec=pltpu.PrefetchScalarGridSpec(
            num_scalar_prefetch=1,
            grid=(RING,),
            in_specs=[pl.BlockSpec((rows, n), lambda k, p: (0, block))] * RING,
            out_specs=spec,
        ),
        out_shape=jax.ShapeDtypeStruct(shape, f32),
        cost_estimate=pl.CostEstimate(flops=0, bytes_accessed=rows * n * RING * 6, transcendentals=0),
    )(place, *pieces)


A, B, CORE, X, DOC = range(5)


class Chunk:
    def __init__(self, info_ref, k, count, tok):
        self.info, self.count, self.tok = info_ref, count, tok
        self.ring = lax.rem(info_ref[A] + RING - k, RING)
        self.first = ((self.ring * count + info_ref[B]) * 2 + info_ref[CORE]) * tok
        self.shift = info_ref[X] * (tok // 2)

    def docs(self):
        return [self.info[DOC + i] for i in range(self.info.shape[0] - DOC)]

    def begin(self, place):
        best = place * 0
        for d in self.docs():
            best = jnp.maximum(best, jnp.where(place >= d, d, 0))
        return best

    def places(self, shape, dim):
        n = lax.broadcasted_iota(jnp.int32, shape, dim)
        n = lax.rem(n, self.tok)
        return self.first + n + jnp.where(n < self.tok // 2, self.shift, -self.shift)

    def keys(self, first_key, n):
        row = lax.broadcasted_iota(jnp.int32, (n, 1), 0)
        within = lax.rem(row, self.tok)
        return first_key + row + jnp.where(within < self.tok // 2, self.shift, -self.shift)

    def quarter(self, i, quarter):
        core = self.info[CORE] if i < 2 else 1 - self.info[CORE]
        side = self.info[B] if self.count == 2 else 0
        side = side if i % 2 == 0 else 1 - side
        return pl.ds(pl.multiple_of((core * 2 + side) * quarter, quarter), quarter)


def row_quarter(at, mine_ref, other_ref, i, quarter):
    cols = at.quarter(i, quarter)
    return jnp.concatenate([mine_ref[:, cols], other_ref[:, cols]], axis=0)


def store_quarter(at, mine_ref, other_ref, i, value):
    half, quarter = value.shape[0] // 2, value.shape[1]
    cols = at.quarter(i, quarter)
    value = value.astype(mine_ref.dtype)
    mine_ref[:, cols] = value[:half]
    other_ref[:, cols] = value[half:]


def rotate(values, cosine, sine):
    half = values.shape[1] // 2
    first, second = values[:, :half], values[:, half:]
    return jnp.concatenate([first * cosine - second * sine, second * cosine + first * sine], axis=1)


def head_norm(values):
    inverse = lax.rsqrt(jnp.mean(values * values, axis=1, keepdims=True) + epsilon)
    return values * inverse, inverse


def head_norm_back(grad_out, gain, unit, inverse):
    scaled = grad_out * gain
    inner_mean = jnp.mean(scaled * unit, axis=1, keepdims=True)
    return inverse * (scaled - unit * inner_mean)


def heads_to_lanes(array, head):
    return jnp.concatenate([array[i : i + head] for i in range(0, array.shape[0], head)], axis=1)


def lanes_to_heads(array, tok):
    return jnp.concatenate([array[:, i : i + tok] for i in range(0, array.shape[1], tok)], axis=0)


def project_kernel(k, count, info_ref, mine_ref, other_ref, w0, w1, w2, w3, qg_ref, kg_ref, q_ref, kv_ref, raw_ref, cos_ref, sin_ref):
    head = qg_ref.shape[0]
    tok = cos_ref.shape[1]
    at = Chunk(info_ref, k, count, tok)
    place = at.places((1, tok), 1)
    turn = lax.broadcasted_iota(jnp.int32, (head // 2, 1), 0).astype(f32) * (2.0 / head)
    turned = (1.0 / rope_base**turn) * (place - at.begin(place)).astype(f32)
    cos_ref[...] = jnp.cos(turned)
    sin_ref[...] = jnp.sin(turned)
    q_n = q_ref.shape[0]
    total = 0.0
    for i, w in enumerate((w0, w1, w2, w3)):
        rows = row_quarter(at, mine_ref, other_ref, i, w.shape[0])
        total = total + jnp.dot(rows, w[:, : raw_ref.shape[0]], preferred_element_type=f32)
    raw = total.T
    raw_ref[...] = raw
    cosine, sine = cos_ref[...], sin_ref[...]
    q_unit, _ = head_norm(raw[:q_n].reshape(q_n // head, head, tok))
    q_ref[...] = rotate(q_unit * qg_ref[...], cosine, sine).reshape(q_n, tok).astype(bf16)
    k_unit, _ = head_norm(raw[q_n + head :].reshape(1, head, tok))
    key = rotate(k_unit * kg_ref[...], cosine, sine).reshape(head, tok)
    kv_ref[...] = jnp.concatenate([raw[q_n : q_n + head], key], axis=0).T.astype(bf16)


def key_loop(at, lanes, step):
    size = PAIR * at.tok
    place = at.places((1, lanes), 1)
    start = at.begin(place)
    high = at.begin(at.first + at.tok - 1)

    def masked(j, scores):
        key = at.keys(j * size, size)
        return jnp.where((key <= place) & (key >= start), scores, NEG)

    def body(j, carry):
        need = ((j + 1) * size > at.first) | (j * size < high)
        pl.when(need)(lambda: step(j, masked))
        pl.when(jnp.logical_not(need))(lambda: step(j, lambda j, scores: scores))
        return carry

    lax.fori_loop(at.begin(at.first) // size, (at.first + at.tok + size - 1) // size, body, 0)


def key_rows(kv_ref, j):
    return kv_ref[pl.ds(j * PAIR, PAIR)].reshape(PAIR * kv_ref.shape[1], kv_ref.shape[2])


def attend_kernel(
    scale, k, count, info_ref, q_ref, kv_ref, w0, w1, w2, w3,
    mixed_ref, lse_ref, low_ref, mine_ref, other_ref, acc, total
):
    head = kv_ref.shape[2] // 2
    tok = q_ref.shape[1]
    at = Chunk(info_ref, k, count, tok)
    acc[...] = jnp.zeros_like(acc)
    total[...] = jnp.zeros_like(total)
    q = heads_to_lanes(q_ref[...], head)
    q = jnp.concatenate([jnp.zeros_like(q), q], axis=0)
    size = PAIR * tok

    def step(j, masked):
        kv = key_rows(kv_ref, j)
        scores = jnp.dot(kv, q, preferred_element_type=f32) * (scale * LOG2E)
        scores = masked(j, scores)
        weights = jnp.exp2(scores)
        total[...] += jnp.sum(weights.reshape(size // 8, 8, -1), axis=0)
        acc[...] += lax.dot_general(
            kv, weights.astype(bf16), (((0,), (0,)), ((), ())), preferred_element_type=f32
        )

    key_loop(at, q.shape[1], step)
    row_total = jnp.sum(total[...], axis=0, keepdims=True)
    lse_ref[...] = jnp.log2(row_total)
    mixed = acc[0:head, :] / row_total
    mixed_ref[...] = mixed
    low = lanes_to_heads(mixed, tok).T.astype(bf16)
    low_ref[...] = low
    for i, w in enumerate((w0, w1, w2, w3)):
        store_quarter(at, mine_ref, other_ref, i, dot(low, w[:, w.shape[1] - low.shape[1] :], 1, 1))


def attend_back_kernel(
    scale, k, count, info_ref, gm_ref, go_ref, w0, w1, w2, w3, q_ref, kv_ref, lse_ref, mixed_ref,
    raw_ref, cos_ref, sin_ref, qg_ref, dkv_in, gq_ref, gain_ref, dkv, acc
):
    head = kv_ref.shape[2] // 2
    q_n, tok = q_ref.shape
    at = Chunk(info_ref, k, count, tok)
    acc[...] = jnp.zeros_like(acc)
    if dkv_in is None:
        dkv[...] = jnp.zeros_like(dkv)
    else:
        dkv[...] = dkv_in[...]
    total = 0.0
    for i, w in enumerate((w0, w1, w2, w3)):
        rows = row_quarter(at, gm_ref, go_ref, i, w.shape[0])
        total = total + jnp.dot(rows, w[:, w.shape[1] - q_n :], preferred_element_type=f32)
    g = heads_to_lanes(total.T.astype(bf16), head)
    delta = jnp.sum(g.astype(f32) * mixed_ref[...], axis=0, keepdims=True)
    g = jnp.concatenate([g, jnp.zeros_like(g)], axis=0)
    q = heads_to_lanes(q_ref[...], head)
    q = jnp.concatenate([jnp.zeros_like(q), q], axis=0)
    lse = lse_ref[...]
    size = PAIR * tok

    def step(j, masked):
        kv = key_rows(kv_ref, j)
        scores = jnp.dot(kv, q, preferred_element_type=f32) * (scale * LOG2E)
        scores = masked(j, scores)
        probs = jnp.exp2(scores - lse)
        grad_probs = jnp.dot(kv, g, preferred_element_type=f32)
        grad_scores = (probs * (grad_probs - delta)).astype(bf16)
        grad_kv = dot(probs.astype(bf16), g, 1, 1) + dot(grad_scores, q, 1, 1)
        dkv[pl.ds(j * PAIR, PAIR)] += grad_kv.reshape(PAIR, tok, -1)
        acc[...] += lax.dot_general(
            kv, grad_scores, (((0,), (0,)), ((), ())), preferred_element_type=f32
        )

    key_loop(at, q.shape[1], step)
    grad = lanes_to_heads(acc[head:, :] * scale, tok).reshape(q_n // head, head, tok)
    grad = rotate(grad, cos_ref[...], -sin_ref[...])
    unit, inverse = head_norm(raw_ref[0:q_n].reshape(q_n // head, head, tok))
    gain_ref[...] = jnp.sum(grad * unit, axis=0)
    gq_ref[...] = head_norm_back(grad, qg_ref[...], unit, inverse).reshape(q_n, tok).T.astype(bf16)


def first_back(*refs):
    attend_back_kernel(*refs[:18], None, *refs[18:])


def project_back_kernel(
    scale, k, count, info_ref, gkv_ref, gq_ref, raw_ref, cos_ref, sin_ref, kg_ref, w0, w1, w2, w3,
    gproj_ref, gain_ref, mine_ref, other_ref
):
    head = kg_ref.shape[0]
    tok, q_n = gq_ref.shape
    at = Chunk(info_ref, k, count, tok)
    gkv = gkv_ref[...].T
    grad = rotate((gkv[head:] * scale).reshape(1, head, tok), cos_ref[...], -sin_ref[...])
    unit, inverse = head_norm(raw_ref[q_n + head : q_n + 2 * head].reshape(1, head, tok))
    gain_ref[...] = jnp.sum(grad * unit, axis=0)
    gk = head_norm_back(grad, kg_ref[...], unit, inverse).reshape(head, tok)
    rest = jnp.concatenate([gkv[:head], gk], axis=0).T.astype(bf16)
    gproj = jnp.concatenate([gq_ref[...], rest], axis=1)
    gproj_ref[...] = gproj
    for i, w in enumerate((w0, w1, w2, w3)):
        store_quarter(at, mine_ref, other_ref, i, dot(gproj, w[:, : gproj.shape[1]], 1, 1))


def feed_kernel(
    k, count, step, info_ref, hm_ref, ho_ref, cm_ref, co_ref,
    p0, p1, p2, p3, d0, d1, d2, d3, *refs
):
    act_ref, sm_ref, so_ref, bm_ref, bo_ref, h_rows, c_rows, *turned = refs[-10:]
    half = hm_ref.shape[0]
    at = Chunk(info_ref, k, count, 2 * half)
    quarter, width = d0.shape
    pairs, downs = (p0, p1, p2, p3), (d0, d1, d2, d3)
    for rows, mine_ref, other_ref in ((h_rows, hm_ref, ho_ref), (c_rows, cm_ref, co_ref)):
        rows[0:half] = mine_ref[...]
        rows[half:] = other_ref[...]

    def product(rows, weights, first):
        cols, total = pl.ds(pl.multiple_of(first, step), step), 0.0
        for i, w in enumerate(weights):
            total = total + jnp.dot(rows[:, at.quarter(i, quarter)], w[:, cols], preferred_element_type=f32)
        return total

    def ahead(j, carry):
        cols = pl.ds(pl.multiple_of(j * step, step), step)
        gate, up = product(h_rows, pairs, j * step), product(h_rows, pairs, width + j * step)
        back = product(c_rows, downs, j * step)
        sigmoid = 1.0 / (1.0 + jnp.exp(-gate))
        silu = gate * sigmoid
        hidden = (silu * up).astype(bf16)
        grad_gate = (back * up * sigmoid * (1.0 + gate * (1.0 - sigmoid))).astype(bf16)
        grad_up = (back * silu).astype(bf16)
        for n, (value, turn_ref) in enumerate(zip((grad_gate, grad_up, hidden), turned)):
            act_ref[:, pl.ds(pl.multiple_of(n * width + j * step, step), step)] = value
            turn_ref[cols, :] = value.T
        return carry

    lax.fori_loop(0, width // step, ahead, 0)
    grad_gate, grad_up, hidden = (ref[...] for ref in turned)
    for i in range(QUARTERS):
        second = jnp.dot(pairs[i][:, :width], grad_gate, preferred_element_type=f32)
        second = second + jnp.dot(pairs[i][:, width:], grad_up, preferred_element_type=f32)
        store_quarter(at, sm_ref, so_ref, i, second.T)
        branch = jnp.dot(downs[i][...], hidden, preferred_element_type=f32)
        store_quarter(at, bm_ref, bo_ref, i, branch.T)


def half_rows(ref, x):
    half = ref.shape[0] // 2
    return pl.ds(pl.multiple_of(x * half, half), half)


def reorder(ref, rows, order, width):
    value = ref[rows, :] if rows is not None else ref[...]
    size = width // len(order)
    return jnp.concatenate([value[:, n * size : (n + 1) * size] for n in order], axis=1)


def enter_kernel(order, info_ref, in_ref, gain_ref, own_ref, unit_ref, inverse_ref, low_ref, other_ref):
    width = in_ref.shape[1]
    gain = reorder(gain_ref, None, order, width)
    for x, low in ((info_ref[X], low_ref), (1 - info_ref[X], other_ref)):
        rows = reorder(in_ref, half_rows(in_ref, x), order, width).astype(f32)
        unit, inverse = norm_rows(rows)
        low[...] = (unit * gain).astype(bf16)
        if low is low_ref:
            own_ref[...] = rows
            unit_ref[...] = unit
            inverse_ref[...] = jnp.broadcast_to(inverse, inverse_ref.shape)


def reorder_kernel(order, info_ref, in_ref, one_ref, two_ref, own_ref, other_ref, gain_one_ref, gain_two_ref):
    width = in_ref.shape[1]
    own_ref[...] = reorder(in_ref, half_rows(in_ref, info_ref[X]), order, width)
    other_ref[...] = reorder(in_ref, half_rows(in_ref, 1 - info_ref[X]), order, width)
    gain_one_ref[...] = reorder(one_ref, None, order, width)
    gain_two_ref[...] = reorder(two_ref, None, order, width)


def leave_kernel(order, info_ref, own_ref, other_ref, out_ref):
    width = own_ref.shape[1]
    for x, ref in ((info_ref[X], own_ref), (1 - info_ref[X], other_ref)):
        out_ref[half_rows(out_ref, x), :] = reorder(ref, None, order, width)


def whole(array):
    shape = array.shape
    return pl.BlockSpec(shape, lambda *_: (0,) * len(shape))


def shaped(shape, kind):
    return jax.ShapeDtypeStruct(shape, kind)


def call(kernel, info, operands, results, scratch=(), cost=(0, 0, 0), aliases=None, in_specs=None, out_specs=None, grid=(1,), vmem=20):
    return pl.pallas_call(
        kernel,
        grid_spec=pltpu.PrefetchScalarGridSpec(
            num_scalar_prefetch=1,
            grid=grid,
            in_specs=in_specs or [whole(o) for o in operands],
            out_specs=out_specs or [whole(r) for r in results],
            scratch_shapes=list(scratch),
        ),
        out_shape=results,
        input_output_aliases=aliases or {},
        compiler_params=pltpu.CompilerParams(vmem_limit_bytes=vmem << 20),
        cost_estimate=pl.CostEstimate(
            flops=cost[0], bytes_accessed=cost[1], transcendentals=cost[2]
        ),
    )(info, *operands)


def shards(
    count,
    inputs,
    norm1_gain,
    query_weight,
    key_weight,
    value_weight,
    query_gain,
    key_gain,
    out_weight,
    norm2_gain,
    gate_weight,
    up_weight,
    down_weight,
    doc_starts,
    cotangent,
):
    at = Place(count)
    links.sent.clear()
    tok, width = inputs.shape
    half = tok // 2
    head = query_gain.shape[0]
    q_n = query_weight.shape[1] // RING
    hidden_n = gate_weight.shape[1] // RING
    heads = q_n // head
    assert key_weight.shape[1] // RING == head
    lanes = heads * tok
    scale = head ** (-0.5)
    blocks = RING * count * 2
    rows = width // blocks

    places = [(i, j, c) for c in range(2) for j in range(count) for i in range(RING)]
    to_order = [(i * count + j) * 2 + c for i, j, c in places]
    to_natural = [to_order.index(n) for n in range(blocks)]

    def natural(array):
        array = array.reshape((2, count, RING, rows))
        return jnp.swapaxes(array, 0, 2).reshape(width)

    def pieces(*arrays):
        stacked = []
        for i in range(RING):
            cut = [m[:, i * (m.shape[1] // RING) : (i + 1) * (m.shape[1] // RING)] for m in arrays]
            stacked.append(jnp.concatenate(cut, axis=1))
        return jnp.stack(stacked)

    info = jnp.concatenate([jnp.stack([at.a, at.b, at.core, at.x]).astype(jnp.int32), doc_starts])
    half_low, half_wide = shaped((half, width), bf16), shaped((half, width), f32)
    row_pair = [half_low] * 2
    query_gain, key_gain = query_gain[:, None], key_gain[:, None]
    gains_natural = [norm1_gain[None], norm2_gain[None]]

    def beside(own):
        if count == 2:
            return [own, swap(own, "b")]
        return jnp.split(lax.all_gather(own, "b", axis=0, tiled=True), 2)

    def quarters(near):
        return list(near) + [swap(part, "core") for part in near]

    side_got = Exchange(at, pieces(query_weight, value_weight, key_weight, out_weight.T)).whole()
    in_own, unit_one, scale_one, h1_own, h1_other = call(
        functools.partial(enter_kernel, to_order),
        info,
        [inputs, gains_natural[0]],
        [half_wide, half_wide, shaped((half, 128), f32), half_low, half_low],
    )
    scale_one = scale_one[:, :1]
    rows_one = RowGather(h1_own, h1_other)
    rows_one.ring()
    first_step = rows_one.mine[1]
    side_near = beside(at.assembled(side_got))
    rows_one.cross()
    rows_one.ring()
    side_w = quarters(side_near)
    rows_one.cross()
    rows_one.ring()
    rows_one.cross()
    h1 = rows_one.chunks()
    pair_x = Exchange(at, pieces(after(gate_weight, first_step), up_weight))
    down_x = Exchange(at, pieces(after(down_weight, rows_one.mine[2]).T))
    q, raw, cosine, sine = ([None] * RING for _ in range(4))
    kv_own = jnp.zeros((RING, tok, 2 * head), bf16)
    for k in range(RING):
        q[k], kv_k, raw[k], cosine[k], sine[k] = call(
            functools.partial(project_kernel, k, count),
            info,
            [*h1[k], *side_w, query_gain, key_gain],
            [
                shaped((q_n, tok), bf16),
                shaped((tok, 2 * head), bf16),
                shaped((q_n + 2 * head, tok), f32),
                *[shaped((head // 2, tok), f32)] * 2,
            ],
            cost=(2 * tok * width * (q_n + 2 * head), 3 << 20, 0),
        )
        kv_own = put(kv_own, kv_k, at.back(k))
    pair_x.step(1)
    pair_x.step(3)
    kv_own = after(kv_own, pair_x.got[1])

    pairs = blocks * tok * lanes // 2
    kv = jnp.zeros((RING, count, 2, tok, 2 * head), bf16)
    if count == 2:
        kv_b = jnp.zeros((RING, 2, tok, 2 * head), bf16)
        kv_b = put(put(kv_b, kv_own, None, at.b), swap(kv_own, "b"), None, 1 - at.b)
    else:
        kv_b = lax.all_gather(kv_own, "b", axis=1)
    kv = put(put(kv, kv_b, None, None, at.core), swap(kv_b, "core"), None, None, 1 - at.core)
    kv = kv.reshape(blocks, tok, 2 * head)
    mixed, lse, low = ([None] * RING for _ in range(3))
    attend = RowScatter()
    for n, k in enumerate(ORDER):
        mixed[k], lse[k], low[k], *part = call(
            functools.partial(attend_kernel, scale, k, count),
            info,
            [after(q[k], *attend.theirs[: max(0, n - 1)][-1:], *attend.arrived[: max(0, n - 2)]), kv, *side_w],
            [shaped((head, lanes), f32), shaped((1, lanes), f32), shaped((tok, q_n), bf16), *row_pair],
            [pltpu.VMEM((2 * head, lanes), f32), pltpu.VMEM((8, lanes), f32)],
            (pairs * 2 * head * 8, 3 << 20, pairs),
        )
        attend.cross(*part)
        if n < RING - 1:
            attend.ring()
            if n < 2:
                pair_x.step(2)
    middle = in_own + attend.sum(RING - 1)
    unit_two, scale_two = norm_rows(middle)
    pair_near = beside(at.assembled(pair_x.got))
    cot_own, cot_other, gain_one, gain_two = call(
        functools.partial(reorder_kernel, to_order),
        info,
        [after(cotangent, kv_own), *gains_natural],
        [half_low, half_low] + [shaped((1, width), f32)] * 2,
    )

    down_x.step(1)
    down_x.step(3)
    rows_two = RowGather((unit_two * gain_two).astype(bf16))
    rows_cot = RowGather(cot_own, cot_other)
    rows_two.ring()
    rows_two.cross()
    down_x.step(2)
    down_x.step(2)
    down_near = beside(at.assembled(down_x.got))
    for _ in range(1, RING):
        rows_cot.ring()
        rows_two.cross()
        if len(rows_two.mine) < RING:
            rows_two.ring()
        rows_cot.cross()
    h2, cot = rows_two.chunks(), rows_cot.chunks()
    feed_w = quarters(pair_near) + quarters(down_near)

    step = min(512, hidden_n)
    offsets = at.offsets(width)

    def tokens(parts):
        return jnp.concatenate([piece for k in ORDER for piece in parts[k]], axis=0)

    def in_order(parts):
        return jnp.concatenate([parts[k] for k in ORDER], axis=0)

    def left_quarters(left):
        return [lax.dynamic_slice(left, (0, o), (left.shape[0], width // QUARTERS)) for o in offsets]

    def over_cores(left, right):
        theirs = [swap(dot(part, right, 0, 0).astype(bf16), "core") for part in left[2:]]
        total = [dot(part, right, 0, 0) + t.astype(f32) for part, t in zip(left[:2], theirs)]
        return (total[0], total[1].astype(bf16)), theirs

    def over_b(own, far):
        if count == 2:
            over_b.events.append(swap(far, "b"))
            total = own + over_b.events[-1].astype(f32)
        else:
            both = jnp.concatenate([own.astype(bf16), far], axis=0).reshape(count, RING * rows, -1)
            total = lax.psum_scatter(both, "b", scatter_dimension=0, tiled=False)
        return total.astype(bf16).reshape(RING, rows, -1)

    second = RowScatter()
    branch = [None] * RING
    act = None
    row_specs = [whole(half_low)] * 2
    for n, k in enumerate(ORDER):
        operands = [after(h2[k][0], *second.theirs[: max(0, n - 1)][-1:], *second.arrived[: max(0, n - 2)]), h2[k][1], *cot[k], *feed_w]
        specs, aliases = row_specs * 2 + [pl.BlockSpec(memory_space=pltpu.VMEM)] * (2 * QUARTERS), None
        if act is not None:
            operands.append(act)
            specs = specs + [pl.BlockSpec(memory_space=pl.ANY)]
            aliases = {len(operands): 0}
        act, *part = call(
            functools.partial(feed_kernel, k, count, step),
            info,
            operands,
            [shaped((RING * tok, 3 * hidden_n), bf16), *row_pair, *row_pair],
            [pltpu.VMEM((tok, width), bf16)] * 2 + [pltpu.VMEM((hidden_n, tok), bf16)] * 3,
            (12 * tok * width * hidden_n, 15 << 20, tok * hidden_n),
            aliases,
            specs,
            [pl.BlockSpec((tok, 3 * hidden_n), lambda j, _, n=n: (n, 0))] + row_specs * 2,
        )
        branch[k] = part[2:]
        second.cross(*part[:2])
        if n < RING - 1:
            second.ring()
    h2_q, cot_q = left_quarters(tokens(h2)), left_quarters(tokens(cot))
    act_due = ((), (), ())
    sums, events = [], []
    for n, left in enumerate((h2_q, h2_q, cot_q)):
        both, theirs = over_cores(left, after(act, *act_due[n])[:, n * hidden_n : (n + 1) * hidden_n])
        sums.append(both)
        events.append(theirs)
    grad_second = second.sum(RING - 1)
    over_b.events = []
    gate_own = over_b(*sums[0])

    grad_middle = cot_own.astype(f32) + norm_back(grad_second, gain_two, unit_two, scale_two)
    gain_two_term = jnp.sum(grad_second * unit_two, axis=0)
    rows_att = RowGather(grad_middle.astype(bf16))
    rows_att.all()
    grad_att = rows_att.chunks()
    up_own = over_b(*sums[1])
    down_own = over_b(*sums[2])
    gate_x, up_x, down_x = Exchange(at, gate_own), Exchange(at, up_own), Exchange(at, down_own)
    late = RowScatter()
    grad_kv, gq, q_gain_term = None, [None] * RING, 0.0
    for k in range(RING):
        operands = [after(grad_att[k][0], *([(), (), *[(e,) for e in over_b.events[:2]]] if count == 2 else [()] * RING)[k]), grad_att[k][1], *side_w, q[k], kv, lse[k], mixed[k], raw[k], cosine[k], sine[k], query_gain]
        kernel, aliases = first_back, None
        if grad_kv is not None:
            kernel, aliases = attend_back_kernel, {len(operands) + 1: 2}
            operands.append(grad_kv)
        gq[k], term, grad_kv = call(
            functools.partial(kernel, scale, k, count),
            info,
            operands,
            [shaped((tok, q_n), bf16), shaped((head, tok), f32), shaped((blocks, tok, 2 * head), f32)],
            [pltpu.VMEM((2 * head, lanes), f32)],
            (pairs * 2 * head * 20, 6 << 20, pairs),
            aliases,
            vmem=20 if blocks * tok <= 4096 else 48,
        )
        q_gain_term = q_gain_term + term
        late.cross(*branch[ORDER[k]])
    gate_due, up_due = gate_x.steps(), up_x.steps()
    for _ in range(RING - 1):
        late.ring()

    grad_kv = after(grad_kv, *over_b.events[2:3]).reshape(RING, count, 2, tok, 2 * head)
    theirs = swap(take(grad_kv, None, None, 1 - at.core).astype(bf16), "core")
    grad_kv = take(grad_kv, None, None, at.core) + theirs.astype(f32)
    if count == 2:
        theirs = swap(take(grad_kv, None, 1 - at.b).astype(bf16), "b")
        grad_kv = take(grad_kv, None, at.b) + theirs.astype(f32)
    else:
        grad_kv = lax.psum_scatter(grad_kv.astype(bf16), "b", scatter_dimension=1, tiled=False).astype(f32)
    out_sum, _ = over_cores(left_quarters(tokens(grad_att)), in_order(low))
    out_own = over_b(*out_sum)
    gproj, k_gain_term = [None] * RING, 0.0
    first = RowScatter()
    for n, k in enumerate(ORDER):
        gproj[k], term, *part = call(
            functools.partial(project_back_kernel, scale, k, count),
            info,
            [take(grad_kv, at.back(k)), gq[k], raw[k], cosine[k], sine[k], key_gain, *side_w],
            [shaped((tok, q_n + 2 * head), bf16), shaped((head, tok), f32), *row_pair],
            cost=(2 * tok * width * (q_n + 2 * head), 3 << 20, 0),
        )
        first.cross(*part)
        k_gain_term = k_gain_term + term
        if n < RING - 1:
            first.ring()
    down_x.steps()
    proj_sum, _ = over_cores(left_quarters(tokens([(after(m, gq[0]), o) for m, o in h1])), in_order(gproj))
    out_got = Exchange(at, out_own).whole()
    proj_got = Exchange(at, over_b(*proj_sum)).whole()

    def leave(own):
        return call(
            functools.partial(leave_kernel, to_natural), info, [own, swap(own, "tp")], [shaped((tok, width), bf16)]
        )[0]

    output = leave((middle + late.sum(RING - 1)).astype(bf16))
    grad_first = first.sum(RING - 1)
    input_grad = (grad_middle + norm_back(grad_first, gain_one, unit_one, scale_one)).astype(bf16)
    gain_one_term = jnp.sum(grad_first * unit_one, axis=0)
    gains = at.sum_everywhere(
        jnp.concatenate([gain_one_term, gain_two_term, jnp.sum(q_gain_term, axis=1), jnp.sum(k_gain_term, axis=1)])
    )
    input_grad = leave(input_grad)
    proj_all = at.assembled(proj_got).reshape(RING, rows, -1)

    def held(values, event):
        return [values[0], *after_all(values[1:], event)]

    def side(first_col, n):
        return jnp.concatenate([proj_all[i, :, first_col : first_col + n] for i in range(RING)], axis=1).astype(f32)

    return (
        output,
        input_grad,
        natural(gains[:width]),
        side(0, q_n),
        side(q_n + head, head),
        side(q_n, head),
        gains[2 * width : 2 * width + head],
        gains[2 * width + head :],
        lay(held(out_got, first.arrived[2]), info, 0, q_n, True),
        natural(gains[width : 2 * width]),
        lay(held(gate_x.got, first.arrived[2]), info, 0, hidden_n, False),
        lay(held(up_x.got, first.arrived[2]), info, 0, hidden_n, False),
        lay(down_x.got, info, 0, hidden_n, True),
    )


def solution(mesh):
    context, tensor = mesh.devices.shape
    count = context // (2 * RING)
    fine = Mesh(mesh.devices.reshape(RING, count, 2, tensor), ("a", "b", "core", "tp"))
    ctx = ("a", "b", "core")
    rows, both, turned = P(ctx, None), P(ctx, "tp"), P("tp", ctx)
    return jax.shard_map(
        functools.partial(shards, count),
        mesh=fine,
        in_specs=(rows, P(), both, both, both, P(), P(), turned, P(), both, both, turned, P(), rows),
        out_specs=(rows, rows, P(), both, both, both, P(), P(), turned, P(), both, both, turned),
        check_vma=False,
    )
```

```python
import functools

import jax
import jax.numpy as jnp
from jax import lax
from jax.experimental import pallas as pl
from jax.experimental.pallas import tpu as pltpu
from jax.sharding import Mesh
from jax.sharding import PartitionSpec as P

epsilon = 1e-05
rope_base = 1000000.0
RING = 4
QUARTERS = 4
ORDER = (1, 2, 3, 0)
LOG2E = 1.4426950408889634
NEG = -1e30
PAIR = 4
DEPTH = {"a": 2, "b": 1, "tp": 1}
bf16 = jnp.bfloat16
f32 = jnp.float32


def norm_rows(values):
    inverse = lax.rsqrt(jnp.mean(values * values, axis=-1, keepdims=True) + epsilon)
    return values * inverse, inverse


def norm_back(grad_out, gain, unit_rows, inverse):
    scaled = grad_out * gain
    inner_mean = jnp.mean(scaled * unit_rows, axis=-1, keepdims=True)
    return inverse * (scaled - unit_rows * inner_mean)


def dot(left, right, left_dim, right_dim):
    return lax.dot_general(
        left, right, (((left_dim,), (right_dim,)), ((), ())), preferred_element_type=f32
    )


class Links:
    def __init__(self):
        self.sent = {}

    def send(self, link, values, move):
        sent = self.sent.setdefault(link, [])
        if len(sent) >= DEPTH[link]:
            values = lax.optimization_barrier((*values, *sent[-DEPTH[link]]))[: len(values)]
        sent.append(tuple(move(i, value) for i, value in enumerate(values)))
        return sent[-1]


links = Links()


def ring_permute(value, step):
    return lax.ppermute(value, "a", [(i, (i + step) % RING) for i in range(RING)])


def ring_shift(value, step):
    return links.send("a", [value], lambda _, v: ring_permute(v, step))[0]


def swap(value, axis):
    def move(_, v):
        return lax.ppermute(v, axis, [(0, 1), (1, 0)])

    return move(0, value) if axis == "core" else links.send(axis, [value], move)[0]


def after(value, *events):
    return lax.optimization_barrier((value,) + events)[0]


def after_all(values, *events):
    return list(lax.optimization_barrier((*values, *events))[: len(values)])


def window(buffer, index):
    start = [0 if i is None else i for i in index] + [0] * (buffer.ndim - len(index))
    shape = [buffer.shape[d] if i is None else 1 for d, i in enumerate(index)]
    return start, shape + list(buffer.shape[len(index) :])


def put(buffer, value, *index):
    start, shape = window(buffer, index)
    return lax.dynamic_update_slice(buffer, value.reshape(shape), start)


def take(buffer, *index):
    start, shape = window(buffer, index)
    kept = [buffer.shape[d] for d, i in enumerate(index) if i is None]
    return lax.dynamic_slice(buffer, start, shape).reshape(kept + list(buffer.shape[len(index) :]))


class Place:
    def __init__(self, count):
        self.a, self.b, self.core, self.x = (lax.axis_index(n) for n in ("a", "b", "core", "tp"))
        self.count = count

    def back(self, k):
        return (self.a - k) % RING

    def ahead(self, k):
        return (self.a + k) % RING

    def assembled(self, pieces):
        own = jnp.zeros((RING,) + pieces[0].shape, pieces[0].dtype)
        for k in range(RING):
            own = put(own, pieces[k], self.back(k))
        return own.reshape(-1, own.shape[-1])

    def over_b_rows(self, own):
        return swap(own, "b")

    def offsets(self, width):
        quarter = width // QUARTERS
        first = self.b if self.count == 2 else 0
        return [(c * 2 + h) * quarter for c in (self.core, 1 - self.core) for h in (first, 1 - first)]

    def over_b(self, array):
        if self.count == 2:
            theirs = swap(take(array, 1 - self.b).astype(bf16), "b")
            return take(array, self.b) + theirs.astype(f32)
        return lax.psum_scatter(array.astype(bf16), "b", scatter_dimension=0, tiled=False).astype(f32)

    def sum_everywhere(self, value):
        def tree(values):
            while len(values) > 1:
                values = [values[i] + values[i + 1] for i in range(0, len(values), 2)]
            return values[0]

        value = value + swap(value, "core")
        if self.count == 2:
            axes = ("b", "tp")
            value = tree([value] + [lax.ppermute(value, axes, [(i, i ^ m) for i in range(4)]) for m in (1, 2, 3)])
        else:
            value = lax.psum(value, "b")
            value = value + lax.ppermute(value, "tp", [(0, 1), (1, 0)])
        return tree([value] + [lax.ppermute(value, "a", [(i, i ^ m) for i in range(RING)]) for m in range(1, RING)])


class RowGather:
    def __init__(self, own, other=None):
        self.mine, self.other = [own], [] if other is None else [other]

    def ring(self, *due):
        self.mine.append(ring_shift(after(self.mine[-1], *due) if due else self.mine[-1], 1))

    def cross(self, k=None):
        k = len(self.other) if k is None else k
        self.other += [None] * (k + 1 - len(self.other))
        self.other[k] = swap(self.mine[k], "tp")

    def all(self):
        for _ in range(1, RING):
            self.ring()
            self.cross()
        if len(self.other) < RING:
            self.cross()
        return self

    def chunks(self):
        return list(zip(self.mine, self.other))


class RowScatter:
    def __init__(self):
        self.totals, self.theirs, self.arrived = [], [], []

    def cross(self, mine, other):
        self.theirs.append(swap(other, "tp"))
        self.totals.append(mine.astype(f32) + self.theirs[-1].astype(f32))

    def ring(self):
        n = len(self.arrived)
        self.arrived.append(ring_shift(self.sum(n).astype(bf16), 1))

    def sum(self, n):
        return self.totals[n] + self.arrived[n - 1].astype(f32) if n else self.totals[0]


class Exchange:
    def __init__(self, at, parts):
        self.at, self.parts, self.got, self.hop = at, parts, [take(parts, at.a), None, None, None], None

    def piece(self, k):
        return take(self.parts, self.at.ahead(k))

    def step(self, k):
        if k != 2:
            self.got[k] = ring_shift(self.piece(k), k)
            return
        if self.hop is None:
            self.hop = ring_shift(self.piece(2), 1)
        else:
            self.got[2] = ring_shift(self.hop, 1)

    def steps(self):
        for k in (1, 3, 2, 2):
            self.step(k)
        return [self.got[1], self.got[3], self.hop, self.got[2]]

    def whole(self):
        got = links.send("a", [self.piece(k) for k in (1, 2, 3)], lambda i, v: ring_permute(v, i + 1))
        self.got[1:] = got
        return self.got


def lay_kernel(turned, place_ref, *refs):
    pieces, out_ref = refs[:-1], refs[-1]
    for k, piece in enumerate(pieces):

        @pl.when(pl.program_id(0) == k)
        def _(piece=piece):
            value = piece[...].astype(f32)
            out_ref[...] = value.T if turned else value


def lay(pieces, a, first, n, turned):
    rows = pieces[0].shape[0]
    block = first // n
    place = a
    if turned:
        shape, spec = (RING * n, rows), pl.BlockSpec((n, rows), lambda k, p: ((p[0] + RING - k) % RING, 0))
    else:
        shape, spec = (rows, RING * n), pl.BlockSpec((rows, n), lambda k, p: (0, (p[0] + RING - k) % RING))
    return pl.pallas_call(
        functools.partial(lay_kernel, turned),
        grid_spec=pltpu.PrefetchScalarGridSpec(
            num_scalar_prefetch=1,
            grid=(RING,),
            in_specs=[pl.BlockSpec((rows, n), lambda k, p: (0, block))] * RING,
            out_specs=spec,
        ),
        out_shape=jax.ShapeDtypeStruct(shape, f32),
        cost_estimate=pl.CostEstimate(flops=0, bytes_accessed=rows * n * RING * 6, transcendentals=0),
    )(place, *pieces)


A, B, CORE, X, DOC = range(5)


class Chunk:
    def __init__(self, info_ref, k, count, tok):
        self.info, self.count, self.tok = info_ref, count, tok
        self.ring = lax.rem(info_ref[A] + RING - k, RING)
        self.first = ((self.ring * count + info_ref[B]) * 2 + info_ref[CORE]) * tok
        self.shift = info_ref[X] * (tok // 2)

    def docs(self):
        return [self.info[DOC + i] for i in range(self.info.shape[0] - DOC)]

    def begin(self, place):
        best = place * 0
        for d in self.docs():
            best = jnp.maximum(best, jnp.where(place >= d, d, 0))
        return best

    def places(self, shape, dim):
        n = lax.broadcasted_iota(jnp.int32, shape, dim)
        n = lax.rem(n, self.tok)
        return self.first + n + jnp.where(n < self.tok // 2, self.shift, -self.shift)

    def keys(self, first_key, n):
        row = lax.broadcasted_iota(jnp.int32, (n, 1), 0)
        within = lax.rem(row, self.tok)
        return first_key + row + jnp.where(within < self.tok // 2, self.shift, -self.shift)

    def quarter(self, i, quarter):
        core = self.info[CORE] if i < 2 else 1 - self.info[CORE]
        side = self.info[B] if self.count == 2 else 0
        side = side if i % 2 == 0 else 1 - side
        return pl.ds(pl.multiple_of((core * 2 + side) * quarter, quarter), quarter)


def row_quarter(at, mine_ref, other_ref, i, quarter):
    cols = at.quarter(i, quarter)
    return jnp.concatenate([mine_ref[:, cols], other_ref[:, cols]], axis=0)


def store_quarter(at, mine_ref, other_ref, i, value):
    half, quarter = value.shape[0] // 2, value.shape[1]
    cols = at.quarter(i, quarter)
    value = value.astype(mine_ref.dtype)
    mine_ref[:, cols] = value[:half]
    other_ref[:, cols] = value[half:]


def rotate(values, cosine, sine):
    half = values.shape[1] // 2
    first, second = values[:, :half], values[:, half:]
    return jnp.concatenate([first * cosine - second * sine, second * cosine + first * sine], axis=1)


def head_norm(values):
    inverse = lax.rsqrt(jnp.mean(values * values, axis=1, keepdims=True) + epsilon)
    return values * inverse, inverse


def head_norm_back(grad_out, gain, unit, inverse):
    scaled = grad_out * gain
    inner_mean = jnp.mean(scaled * unit, axis=1, keepdims=True)
    return inverse * (scaled - unit * inner_mean)


def heads_to_lanes(array, head):
    return jnp.concatenate([array[i : i + head] for i in range(0, array.shape[0], head)], axis=1)


def lanes_to_heads(array, tok):
    return jnp.concatenate([array[:, i : i + tok] for i in range(0, array.shape[1], tok)], axis=0)


def project_kernel(k, count, info_ref, mine_ref, other_ref, w0, w1, w2, w3, qg_ref, kg_ref, q_ref, kv_ref, raw_ref, cos_ref, sin_ref):
    head = qg_ref.shape[0]
    tok = cos_ref.shape[1]
    at = Chunk(info_ref, k, count, tok)
    place = at.places((1, tok), 1)
    turn = lax.broadcasted_iota(jnp.int32, (head // 2, 1), 0).astype(f32) * (2.0 / head)
    turned = (1.0 / rope_base**turn) * (place - at.begin(place)).astype(f32)
    cos_ref[...] = jnp.cos(turned)
    sin_ref[...] = jnp.sin(turned)
    q_n = q_ref.shape[0]
    total = 0.0
    for i, w in enumerate((w0, w1, w2, w3)):
        rows = row_quarter(at, mine_ref, other_ref, i, w.shape[0])
        total = total + jnp.dot(rows, w[:, : raw_ref.shape[0]], preferred_element_type=f32)
    raw = total.T
    raw_ref[...] = raw
    cosine, sine = cos_ref[...], sin_ref[...]
    q_unit, _ = head_norm(raw[:q_n].reshape(q_n // head, head, tok))
    q_ref[...] = rotate(q_unit * qg_ref[...], cosine, sine).reshape(q_n, tok).astype(bf16)
    k_unit, _ = head_norm(raw[q_n + head :].reshape(1, head, tok))
    key = rotate(k_unit * kg_ref[...], cosine, sine).reshape(head, tok)
    kv_ref[...] = jnp.concatenate([raw[q_n : q_n + head], key], axis=0).T.astype(bf16)


def key_loop(at, lanes, step):
    size = PAIR * at.tok
    place = at.places((1, lanes), 1)
    start = at.begin(place)
    high = at.begin(at.first + at.tok - 1)

    def masked(j, scores):
        key = at.keys(j * size, size)
        return jnp.where((key <= place) & (key >= start), scores, NEG)

    def body(j, carry):
        need = ((j + 1) * size > at.first) | (j * size < high)
        pl.when(need)(lambda: step(j, masked))
        pl.when(jnp.logical_not(need))(lambda: step(j, lambda j, scores: scores))
        return carry

    lax.fori_loop(at.begin(at.first) // size, (at.first + at.tok + size - 1) // size, body, 0)


def key_rows(kv_ref, j):
    return kv_ref[pl.ds(j * PAIR, PAIR)].reshape(PAIR * kv_ref.shape[1], kv_ref.shape[2])


def attend_kernel(
    scale, k, count, info_ref, q_ref, kv_ref, w0, w1, w2, w3,
    mixed_ref, lse_ref, low_ref, mine_ref, other_ref, acc, total
):
    head = kv_ref.shape[2] // 2
    tok = q_ref.shape[1]
    at = Chunk(info_ref, k, count, tok)
    acc[...] = jnp.zeros_like(acc)
    total[...] = jnp.zeros_like(total)
    q = heads_to_lanes(q_ref[...], head)
    q = jnp.concatenate([jnp.zeros_like(q), q], axis=0)
    size = PAIR * tok

    def step(j, masked):
        kv = key_rows(kv_ref, j)
        scores = jnp.dot(kv, q, preferred_element_type=f32) * (scale * LOG2E)
        scores = masked(j, scores)
        weights = jnp.exp2(scores)
        total[...] += jnp.sum(weights.reshape(size // 8, 8, -1), axis=0)
        acc[...] += lax.dot_general(
            kv, weights.astype(bf16), (((0,), (0,)), ((), ())), preferred_element_type=f32
        )

    key_loop(at, q.shape[1], step)
    row_total = jnp.sum(total[...], axis=0, keepdims=True)
    lse_ref[...] = jnp.log2(row_total)
    mixed = acc[0:head, :] / row_total
    mixed_ref[...] = mixed
    low = lanes_to_heads(mixed, tok).T.astype(bf16)
    low_ref[...] = low
    for i, w in enumerate((w0, w1, w2, w3)):
        store_quarter(at, mine_ref, other_ref, i, dot(low, w[:, w.shape[1] - low.shape[1] :], 1, 1))


def attend_back_kernel(
    scale, k, count, info_ref, gm_ref, go_ref, w0, w1, w2, w3, q_ref, kv_ref, lse_ref, mixed_ref,
    raw_ref, cos_ref, sin_ref, qg_ref, dkv_in, gq_ref, gain_ref, dkv, acc
):
    head = kv_ref.shape[2] // 2
    q_n, tok = q_ref.shape
    at = Chunk(info_ref, k, count, tok)
    acc[...] = jnp.zeros_like(acc)
    if dkv_in is None:
        dkv[...] = jnp.zeros_like(dkv)
    else:
        dkv[...] = dkv_in[...]
    total = 0.0
    for i, w in enumerate((w0, w1, w2, w3)):
        rows = row_quarter(at, gm_ref, go_ref, i, w.shape[0])
        total = total + jnp.dot(rows, w[:, w.shape[1] - q_n :], preferred_element_type=f32)
    g = heads_to_lanes(total.T.astype(bf16), head)
    delta = jnp.sum(g.astype(f32) * mixed_ref[...], axis=0, keepdims=True)
    g = jnp.concatenate([g, jnp.zeros_like(g)], axis=0)
    q = heads_to_lanes(q_ref[...], head)
    q = jnp.concatenate([jnp.zeros_like(q), q], axis=0)
    lse = lse_ref[...]
    size = PAIR * tok

    def step(j, masked):
        kv = key_rows(kv_ref, j)
        scores = jnp.dot(kv, q, preferred_element_type=f32) * (scale * LOG2E)
        scores = masked(j, scores)
        probs = jnp.exp2(scores - lse)
        grad_probs = jnp.dot(kv, g, preferred_element_type=f32)
        grad_scores = (probs * (grad_probs - delta)).astype(bf16)
        grad_kv = dot(probs.astype(bf16), g, 1, 1) + dot(grad_scores, q, 1, 1)
        dkv[pl.ds(j * PAIR, PAIR)] += grad_kv.reshape(PAIR, tok, -1)
        acc[...] += lax.dot_general(
            kv, grad_scores, (((0,), (0,)), ((), ())), preferred_element_type=f32
        )

    key_loop(at, q.shape[1], step)
    grad = lanes_to_heads(acc[head:, :] * scale, tok).reshape(q_n // head, head, tok)
    grad = rotate(grad, cos_ref[...], -sin_ref[...])
    unit, inverse = head_norm(raw_ref[0:q_n].reshape(q_n // head, head, tok))
    gain_ref[...] = jnp.sum(grad * unit, axis=0)
    gq_ref[...] = head_norm_back(grad, qg_ref[...], unit, inverse).reshape(q_n, tok).T.astype(bf16)


def first_back(*refs):
    attend_back_kernel(*refs[:18], None, *refs[18:])


def project_back_kernel(
    scale, k, count, info_ref, gkv_ref, gq_ref, raw_ref, cos_ref, sin_ref, kg_ref, w0, w1, w2, w3,
    gproj_ref, gain_ref, mine_ref, other_ref
):
    head = kg_ref.shape[0]
    tok, q_n = gq_ref.shape
    at = Chunk(info_ref, k, count, tok)
    gkv = gkv_ref[...].T
    grad = rotate((gkv[head:] * scale).reshape(1, head, tok), cos_ref[...], -sin_ref[...])
    unit, inverse = head_norm(raw_ref[q_n + head : q_n + 2 * head].reshape(1, head, tok))
    gain_ref[...] = jnp.sum(grad * unit, axis=0)
    gk = head_norm_back(grad, kg_ref[...], unit, inverse).reshape(head, tok)
    rest = jnp.concatenate([gkv[:head], gk], axis=0).T.astype(bf16)
    gproj = jnp.concatenate([gq_ref[...], rest], axis=1)
    gproj_ref[...] = gproj
    for i, w in enumerate((w0, w1, w2, w3)):
        store_quarter(at, mine_ref, other_ref, i, dot(gproj, w[:, : gproj.shape[1]], 1, 1))


def feed_kernel(
    k, count, step, info_ref, hm_ref, ho_ref, cm_ref, co_ref,
    p0, p1, p2, p3, d0, d1, d2, d3, *refs
):
    act_ref, sm_ref, so_ref, bm_ref, bo_ref, h_rows, c_rows, *turned = refs[-10:]
    half = hm_ref.shape[0]
    at = Chunk(info_ref, k, count, 2 * half)
    quarter, width = d0.shape
    pairs, downs = (p0, p1, p2, p3), (d0, d1, d2, d3)
    for rows, mine_ref, other_ref in ((h_rows, hm_ref, ho_ref), (c_rows, cm_ref, co_ref)):
        rows[0:half] = mine_ref[...]
        rows[half:] = other_ref[...]

    def product(rows, weights, first):
        cols, total = pl.ds(pl.multiple_of(first, step), step), 0.0
        for i, w in enumerate(weights):
            total = total + jnp.dot(rows[:, at.quarter(i, quarter)], w[:, cols], preferred_element_type=f32)
        return total

    def ahead(j, carry):
        cols = pl.ds(pl.multiple_of(j * step, step), step)
        gate, up = product(h_rows, pairs, j * step), product(h_rows, pairs, width + j * step)
        back = product(c_rows, downs, j * step)
        sigmoid = 1.0 / (1.0 + jnp.exp(-gate))
        silu = gate * sigmoid
        hidden = (silu * up).astype(bf16)
        grad_gate = (back * up * sigmoid * (1.0 + gate * (1.0 - sigmoid))).astype(bf16)
        grad_up = (back * silu).astype(bf16)
        for n, (value, turn_ref) in enumerate(zip((grad_gate, grad_up, hidden), turned)):
            act_ref[:, pl.ds(pl.multiple_of(n * width + j * step, step), step)] = value
            turn_ref[cols, :] = value.T
        return carry

    lax.fori_loop(0, width // step, ahead, 0)
    grad_gate, grad_up, hidden = (ref[...] for ref in turned)
    for i in range(QUARTERS):
        second = jnp.dot(pairs[i][:, :width], grad_gate, preferred_element_type=f32)
        second = second + jnp.dot(pairs[i][:, width:], grad_up, preferred_element_type=f32)
        store_quarter(at, sm_ref, so_ref, i, second.T)
        branch = jnp.dot(downs[i][...], hidden, preferred_element_type=f32)
        store_quarter(at, bm_ref, bo_ref, i, branch.T)


def half_rows(ref, x):
    half = ref.shape[0] // 2
    return pl.ds(pl.multiple_of(x * half, half), half)


def reorder(ref, rows, order, width):
    value = ref[rows, :] if rows is not None else ref[...]
    size = width // len(order)
    return jnp.concatenate([value[:, n * size : (n + 1) * size] for n in order], axis=1)


def enter_kernel(order, info_ref, in_ref, gain_ref, own_ref, unit_ref, inverse_ref, low_ref, other_ref):
    width = in_ref.shape[1]
    gain = reorder(gain_ref, None, order, width)
    for x, low in ((info_ref[X], low_ref), (1 - info_ref[X], other_ref)):
        rows = reorder(in_ref, half_rows(in_ref, x), order, width).astype(f32)
        unit, inverse = norm_rows(rows)
        low[...] = (unit * gain).astype(bf16)
        if low is low_ref:
            own_ref[...] = rows
            unit_ref[...] = unit
            inverse_ref[...] = jnp.broadcast_to(inverse, inverse_ref.shape)


def reorder_kernel(order, info_ref, in_ref, one_ref, two_ref, own_ref, other_ref, gain_one_ref, gain_two_ref):
    width = in_ref.shape[1]
    own_ref[...] = reorder(in_ref, half_rows(in_ref, info_ref[X]), order, width)
    other_ref[...] = reorder(in_ref, half_rows(in_ref, 1 - info_ref[X]), order, width)
    gain_one_ref[...] = reorder(one_ref, None, order, width)
    gain_two_ref[...] = reorder(two_ref, None, order, width)


def leave_kernel(order, info_ref, own_ref, other_ref, out_ref):
    width = own_ref.shape[1]
    for x, ref in ((info_ref[X], own_ref), (1 - info_ref[X], other_ref)):
        out_ref[half_rows(out_ref, x), :] = reorder(ref, None, order, width)


def whole(array):
    shape = array.shape
    return pl.BlockSpec(shape, lambda *_: (0,) * len(shape))


def shaped(shape, kind):
    return jax.ShapeDtypeStruct(shape, kind)


def call(kernel, info, operands, results, scratch=(), cost=(0, 0, 0), aliases=None, in_specs=None, out_specs=None, grid=(1,), vmem=20):
    return pl.pallas_call(
        kernel,
        grid_spec=pltpu.PrefetchScalarGridSpec(
            num_scalar_prefetch=1,
            grid=grid,
            in_specs=in_specs or [whole(o) for o in operands],
            out_specs=out_specs or [whole(r) for r in results],
            scratch_shapes=list(scratch),
        ),
        out_shape=results,
        input_output_aliases=aliases or {},
        compiler_params=pltpu.CompilerParams(vmem_limit_bytes=vmem << 20),
        cost_estimate=pl.CostEstimate(
            flops=cost[0], bytes_accessed=cost[1], transcendentals=cost[2]
        ),
    )(info, *operands)


def shards(
    count,
    inputs,
    norm1_gain,
    query_weight,
    key_weight,
    value_weight,
    query_gain,
    key_gain,
    out_weight,
    norm2_gain,
    gate_weight,
    up_weight,
    down_weight,
    doc_starts,
    cotangent,
):
    at = Place(count)
    links.sent.clear()
    tok, width = inputs.shape
    half = tok // 2
    head = query_gain.shape[0]
    q_n = query_weight.shape[1] // RING
    hidden_n = gate_weight.shape[1] // RING
    heads = q_n // head
    assert key_weight.shape[1] // RING == head
    lanes = heads * tok
    scale = head ** (-0.5)
    blocks = RING * count * 2
    rows = width // blocks

    places = [(i, j, c) for c in range(2) for j in range(count) for i in range(RING)]
    to_order = [(i * count + j) * 2 + c for i, j, c in places]
    to_natural = [to_order.index(n) for n in range(blocks)]

    def natural(array):
        array = array.reshape((2, count, RING, rows))
        return jnp.swapaxes(array, 0, 2).reshape(width)

    def pieces(*arrays):
        stacked = []
        for i in range(RING):
            cut = [m[:, i * (m.shape[1] // RING) : (i + 1) * (m.shape[1] // RING)] for m in arrays]
            stacked.append(jnp.concatenate(cut, axis=1))
        return jnp.stack(stacked)

    info = jnp.concatenate([jnp.stack([at.a, at.b, at.core, at.x]).astype(jnp.int32), doc_starts])
    half_low, half_wide = shaped((half, width), bf16), shaped((half, width), f32)
    row_pair = [half_low] * 2
    query_gain, key_gain = query_gain[:, None], key_gain[:, None]
    gains_natural = [norm1_gain[None], norm2_gain[None]]

    def beside(own):
        if count == 2:
            return [own, swap(own, "b")]
        return jnp.split(lax.all_gather(own, "b", axis=0, tiled=True), 2)

    def quarters(near):
        return list(near) + [swap(part, "core") for part in near]

    side_got = Exchange(at, pieces(query_weight, value_weight, key_weight, out_weight.T)).whole()
    in_own, unit_one, scale_one, h1_own, h1_other = call(
        functools.partial(enter_kernel, to_order),
        info,
        [inputs, gains_natural[0]],
        [half_wide, half_wide, shaped((half, 128), f32), half_low, half_low],
    )
    scale_one = scale_one[:, :1]
    rows_one = RowGather(h1_own, h1_other)
    rows_one.ring()
    first_step = rows_one.mine[1]
    side_near = beside(at.assembled([side_got[0], *after_all(side_got[1:], first_step)]))
    rows_one.cross()
    rows_one.ring()
    side_w = quarters(side_near)
    rows_one.cross()
    rows_one.ring()
    rows_one.cross()
    h1 = rows_one.chunks()
    pair_x = Exchange(at, pieces(after(gate_weight, first_step), up_weight))
    down_x = Exchange(at, pieces(after(down_weight, rows_one.mine[2]).T))
    q, raw, cosine, sine = ([None] * RING for _ in range(4))
    kv_own = jnp.zeros((RING, tok, 2 * head), bf16)
    for k in range(RING):
        q[k], kv_k, raw[k], cosine[k], sine[k] = call(
            functools.partial(project_kernel, k, count),
            info,
            [*h1[k], *side_w, query_gain, key_gain],
            [
                shaped((q_n, tok), bf16),
                shaped((tok, 2 * head), bf16),
                shaped((q_n + 2 * head, tok), f32),
                *[shaped((head // 2, tok), f32)] * 2,
            ],
            cost=(2 * tok * width * (q_n + 2 * head), 3 << 20, 0),
        )
        kv_own = put(kv_own, kv_k, at.back(k))
    pair_x.step(1)
    pair_x.step(3)
    kv_own = after(kv_own, pair_x.got[1])

    pairs = blocks * tok * lanes // 2
    kv = jnp.zeros((RING, count, 2, tok, 2 * head), bf16)
    if count == 2:
        kv_b = jnp.zeros((RING, 2, tok, 2 * head), bf16)
        kv_b = put(put(kv_b, kv_own, None, at.b), swap(kv_own, "b"), None, 1 - at.b)
    else:
        kv_b = lax.all_gather(kv_own, "b", axis=1)
    kv = put(put(kv, kv_b, None, None, at.core), swap(kv_b, "core"), None, None, 1 - at.core)
    kv = kv.reshape(blocks, tok, 2 * head)
    mixed, lse, low = ([None] * RING for _ in range(3))
    attend = RowScatter()
    for n, k in enumerate(ORDER):
        mixed[k], lse[k], low[k], *part = call(
            functools.partial(attend_kernel, scale, k, count),
            info,
            [after(q[k], *attend.theirs[: max(0, n - 1)][-1:], *attend.arrived[: max(0, n - 2)]), kv, *side_w],
            [shaped((head, lanes), f32), shaped((1, lanes), f32), shaped((tok, q_n), bf16), *row_pair],
            [pltpu.VMEM((2 * head, lanes), f32), pltpu.VMEM((8, lanes), f32)],
            (pairs * 2 * head * 8, 3 << 20, pairs),
        )
        attend.cross(*part)
        if n < RING - 1:
            attend.ring()
            if n < 2:
                pair_x.step(2)
    middle = in_own + attend.sum(RING - 1)
    unit_two, scale_two = norm_rows(middle)
    pair_near = beside(at.assembled(pair_x.got))
    cot_own, cot_other, gain_one, gain_two = call(
        functools.partial(reorder_kernel, to_order),
        info,
        [after(cotangent, kv_own), *gains_natural],
        [half_low, half_low] + [shaped((1, width), f32)] * 2,
    )

    down_x.step(1)
    down_x.step(3)
    rows_two = RowGather((unit_two * gain_two).astype(bf16))
    rows_cot = RowGather(cot_own, cot_other)
    rows_two.ring()
    rows_two.cross()
    down_x.step(2)
    down_x.step(2)
    down_near = beside(at.assembled(down_x.got))
    for _ in range(1, RING):
        rows_cot.ring()
        rows_two.cross()
        if len(rows_two.mine) < RING:
            rows_two.ring()
        rows_cot.cross()
    h2, cot = rows_two.chunks(), rows_cot.chunks()
    feed_w = quarters(pair_near) + quarters(down_near)

    step = min(1024, hidden_n)
    offsets = at.offsets(width)

    def tokens(parts):
        return jnp.concatenate([piece for k in ORDER for piece in parts[k]], axis=0)

    def in_order(parts):
        return jnp.concatenate([parts[k] for k in ORDER], axis=0)

    def left_quarters(left):
        return [lax.dynamic_slice(left, (0, o), (left.shape[0], width // QUARTERS)) for o in offsets]

    def over_cores(left, right):
        theirs = [swap(dot(part, right, 0, 0).astype(bf16), "core") for part in left[2:]]
        total = [dot(part, right, 0, 0) + t.astype(f32) for part, t in zip(left[:2], theirs)]
        return (total[0], total[1].astype(bf16)), theirs

    def over_b(own, far):
        if count == 2:
            over_b.events.append(swap(far, "b"))
            total = own + over_b.events[-1].astype(f32)
        else:
            both = jnp.concatenate([own.astype(bf16), far], axis=0).reshape(count, RING * rows, -1)
            total = lax.psum_scatter(both, "b", scatter_dimension=0, tiled=False)
        return total.astype(bf16).reshape(RING, rows, -1)

    second = RowScatter()
    branch = [None] * RING
    act = None
    row_specs = [whole(half_low)] * 2
    for n, k in enumerate(ORDER):
        operands = [after(h2[k][0], *second.theirs[: max(0, n - 1)][-1:], *second.arrived[: max(0, n - 2)]), h2[k][1], *cot[k], *feed_w]
        specs, aliases = row_specs * 2 + [pl.BlockSpec(memory_space=pltpu.VMEM)] * (2 * QUARTERS), None
        if act is not None:
            operands.append(act)
            specs = specs + [pl.BlockSpec(memory_space=pl.ANY)]
            aliases = {len(operands): 0}
        act, *part = call(
            functools.partial(feed_kernel, k, count, step),
            info,
            operands,
            [shaped((RING * tok, 3 * hidden_n), bf16), *row_pair, *row_pair],
            [pltpu.VMEM((tok, width), bf16)] * 2 + [pltpu.VMEM((hidden_n, tok), bf16)] * 3,
            (12 * tok * width * hidden_n, 15 << 20, tok * hidden_n),
            aliases,
            specs,
            [pl.BlockSpec((tok, 3 * hidden_n), lambda j, _, n=n: (n, 0))] + row_specs * 2,
        )
        branch[k] = part[2:]
        second.cross(*part[:2])
        if n < RING - 1:
            second.ring()
    h2_q, cot_q = left_quarters(tokens(h2)), left_quarters(tokens(cot))
    act_due = ((), (), ())
    sums, events = [], []
    for n, left in enumerate((h2_q, h2_q, cot_q)):
        both, theirs = over_cores(left, after(act, *act_due[n])[:, n * hidden_n : (n + 1) * hidden_n])
        sums.append(both)
        events.append(theirs)
    grad_second = second.sum(RING - 1)
    over_b.events = []
    gate_own = over_b(*sums[0])

    grad_middle = cot_own.astype(f32) + norm_back(grad_second, gain_two, unit_two, scale_two)
    gain_two_term = jnp.sum(grad_second * unit_two, axis=0)
    rows_att = RowGather(grad_middle.astype(bf16))
    for n in range(1, RING):
        rows_att.ring(*((), events[0], events[1])[n - 1])
        rows_att.cross()
    rows_att.cross()
    grad_att = rows_att.chunks()
    up_own = over_b(*sums[1])
    down_own = over_b(*sums[2])
    gate_x, up_x, down_x = Exchange(at, gate_own), Exchange(at, up_own), Exchange(at, down_own)
    late = RowScatter()
    grad_kv, gq, q_gain_term = None, [None] * RING, 0.0
    for k in range(RING):
        operands = [after(grad_att[k][0], *([(), (), *[(e,) for e in over_b.events[:2]]] if count == 2 else [()] * RING)[k]), grad_att[k][1], *side_w, q[k], kv, lse[k], mixed[k], raw[k], cosine[k], sine[k], query_gain]
        kernel, aliases = first_back, None
        if grad_kv is not None:
            kernel, aliases = attend_back_kernel, {len(operands) + 1: 2}
            operands.append(grad_kv)
        gq[k], term, grad_kv = call(
            functools.partial(kernel, scale, k, count),
            info,
            operands,
            [shaped((tok, q_n), bf16), shaped((head, tok), f32), shaped((blocks, tok, 2 * head), f32)],
            [pltpu.VMEM((2 * head, lanes), f32)],
            (pairs * 2 * head * 20, 6 << 20, pairs),
            aliases,
            vmem=20 if blocks * tok <= 4096 else 48,
        )
        q_gain_term = q_gain_term + term
        late.cross(*branch[ORDER[k]])
    gate_due, up_due = gate_x.steps(), up_x.steps()
    for _ in range(RING - 1):
        late.ring()

    grad_kv = after(grad_kv, *over_b.events[2:3]).reshape(RING, count, 2, tok, 2 * head)
    theirs = swap(take(grad_kv, None, None, 1 - at.core).astype(bf16), "core")
    grad_kv = take(grad_kv, None, None, at.core) + theirs.astype(f32)
    if count == 2:
        theirs = swap(take(grad_kv, None, 1 - at.b).astype(bf16), "b")
        grad_kv = take(grad_kv, None, at.b) + theirs.astype(f32)
    else:
        grad_kv = lax.psum_scatter(grad_kv.astype(bf16), "b", scatter_dimension=1, tiled=False).astype(f32)
    out_sum, _ = over_cores(left_quarters(tokens(grad_att)), in_order(low))
    out_own = over_b(*out_sum)
    gproj, k_gain_term = [None] * RING, 0.0
    first = RowScatter()
    for n, k in enumerate(ORDER):
        gproj[k], term, *part = call(
            functools.partial(project_back_kernel, scale, k, count),
            info,
            [take(grad_kv, at.back(k)), gq[k], raw[k], cosine[k], sine[k], key_gain, *side_w],
            [shaped((tok, q_n + 2 * head), bf16), shaped((head, tok), f32), *row_pair],
            cost=(2 * tok * width * (q_n + 2 * head), 3 << 20, 0),
        )
        first.cross(*part)
        k_gain_term = k_gain_term + term
        if n < RING - 1:
            first.ring()
    down_x.steps()
    proj_sum, _ = over_cores(left_quarters(tokens([(after(m, gq[0]), o) for m, o in h1])), in_order(gproj))
    out_got = Exchange(at, out_own).whole()
    proj_got = Exchange(at, over_b(*proj_sum)).whole()

    def leave(own):
        return call(
            functools.partial(leave_kernel, to_natural), info, [own, swap(own, "tp")], [shaped((tok, width), bf16)]
        )[0]

    output = leave((middle + late.sum(RING - 1)).astype(bf16))
    grad_first = first.sum(RING - 1)
    input_grad = (grad_middle + norm_back(grad_first, gain_one, unit_one, scale_one)).astype(bf16)
    gain_one_term = jnp.sum(grad_first * unit_one, axis=0)
    gains = at.sum_everywhere(
        jnp.concatenate([gain_one_term, gain_two_term, jnp.sum(q_gain_term, axis=1), jnp.sum(k_gain_term, axis=1)])
    )
    input_grad = leave(input_grad)
    proj_all = at.assembled(proj_got).reshape(RING, rows, -1)

    def held(values, event):
        return [values[0], *after_all(values[1:], event)]

    def side(first_col, n):
        return jnp.concatenate([proj_all[i, :, first_col : first_col + n] for i in range(RING)], axis=1).astype(f32)

    return (
        output,
        input_grad,
        natural(gains[:width]),
        side(0, q_n),
        side(q_n + head, head),
        side(q_n, head),
        gains[2 * width : 2 * width + head],
        gains[2 * width + head :],
        lay(held(out_got, first.arrived[2]), info, 0, q_n, True),
        natural(gains[width : 2 * width]),
        lay(held(gate_x.got, first.arrived[2]), info, 0, hidden_n, False),
        lay(held(up_x.got, first.arrived[2]), info, 0, hidden_n, False),
        lay(down_x.got, info, 0, hidden_n, True),
    )


def solution(mesh):
    context, tensor = mesh.devices.shape
    count = context // (2 * RING)
    fine = Mesh(mesh.devices.reshape(RING, count, 2, tensor), ("a", "b", "core", "tp"))
    ctx = ("a", "b", "core")
    rows, both, turned = P(ctx, None), P(ctx, "tp"), P("tp", ctx)
    return jax.shard_map(
        functools.partial(shards, count),
        mesh=fine,
        in_specs=(rows, P(), both, both, both, P(), P(), turned, P(), both, both, turned, P(), rows),
        out_specs=(rows, rows, P(), both, both, both, P(), P(), turned, P(), both, both, turned),
        check_vma=False,
    )
```
